32 devices in a mesh: ctx: 8 (over z, core), ch: 4 (over y, x).
Axes of the slice: x: 2, y: 2, z: 4, core: 2. Of those that a mesh axis runs over, the one named last changes fastest.
Arguments:
- query: bfloat16 [1024, 8192], P('ctx', 'ch'), may hold values from -6 to 6
- key: bfloat16 [1024, 8192], P('ctx', 'ch'), may hold values from -6 to 6
- value: bfloat16 [1024, 8192], P('ctx', 'ch'), may hold values from -6 to 6
- cotangent: bfloat16 [1024, 8192], P('ctx', 'ch'), may hold values from -6 to 6
- decay: float32 [4, 8192], P(None, 'ch'), may hold values from 0.95 to 1, as said below
- residue: float32 [4, 8192], P(None, 'ch'), may hold values from -3 to 3
- skip: float32 [8192], P('ch'), may hold values from -4 to 4
Outputs:
- output: bfloat16 [1024, 8192], P('ctx', 'ch')
- query_grad: bfloat16 [1024, 8192], P('ctx', 'ch')
- key_grad: bfloat16 [1024, 8192], P('ctx', 'ch')
- value_grad: bfloat16 [1024, 8192], P('ctx', 'ch')
- residue_grad: float32 [4, 8192], P(None, 'ch')
- skip_grad: float32 [8192], P('ch')
The draws below stay inside these ranges and needn't reach their ends.
Inputs may be any that keep to these rules, and one draw needn't show every extreme that they name: decay lies below 1.
All inputs are finite; a program needn't handle non-finite values.
Results may differ from the reference program's by a relative error of at most 0.0012.
Values sent between devices are 32-bit elements; how exact they have to be, the bound alone decides.
A program may use at most 64 MiB of HBM per device.

```python
import math
import jax
import jax.numpy as jnp
from jax import lax

D = 8192
MODES = 4
SEQ = 1024


def draw_decay(key, part):
    first, second = jax.random.split(key, 2)
    slow_share = 0.5
    slow = jax.random.uniform(first, (MODES, D), jnp.float32) < slow_share
    ratio = jax.random.uniform(second, (MODES, D), jnp.float32)
    slow_low = math.log(0.1 / SEQ)
    slow_high = math.log(2.0 / SEQ)
    fast_high = math.log(0.05)
    slow_rate = jnp.exp(slow_low + ratio * (slow_high - slow_low))
    fast_rate = jnp.exp(slow_high + ratio * (fast_high - slow_high))
    rate = jnp.where(slow, slow_rate, fast_rate)
    return jnp.exp(-rate).astype(jnp.float32)


def steps_of(rng, shape, shards, low, top_value):
    def one(dim, parts):
        draws = jax.random.uniform(jax.random.fold_in(jax.random.fold_in(rng, 6), dim), (parts,), jnp.float32, low / len(shards), top_value / len(shards))
        return jnp.repeat(jnp.exp(draws), shape[dim] // parts).reshape((-1,) + (1,) * (len(shape) - dim - 1))

    level = one(*shards[0])
    for cut in shards[1:]:
        level = level * one(*cut)
    return level


def bell_draw(own_key, dims, scale, limit, cuts=(), kind=jnp.bfloat16):
    result = scale * jax.random.normal(own_key, dims, jnp.float32)
    if cuts:
        result = result * steps_of(own_key, dims, cuts, -0.22, 0.18)
    return jnp.clip(result, -limit, limit).astype(kind)


def setup_inputs(seed: int = 0) -> dict:
    arg_keys = jax.random.split(jax.random.key(seed), 8)
    return {
        "query": bell_draw(arg_keys[0], (SEQ, D), 1.0, 6.0, ((0, 8), (1, 4))),
        "key": bell_draw(arg_keys[1], (SEQ, D), 1.0, 6.0, ((0, 8), (1, 4))),
        "value": bell_draw(arg_keys[2], (SEQ, D), 1.0, 6.0, ((0, 8), (1, 4))),
        "cotangent": bell_draw(arg_keys[3], (SEQ, D), 1.0, 6.0, ((0, 8), (1, 4))),
        "decay": draw_decay(jax.random.fold_in(arg_keys[7], 71), 0),
        "residue": bell_draw(arg_keys[5], (MODES, D), 0.5, 3.0, ((1, 4),), jnp.float32),
        "skip": bell_draw(arg_keys[6], (D,), 1.0, 4.0, ((0, 4),), jnp.float32),
    }


def reference(query, key, value, cotangent, decay, residue, skip):
    inner = key.astype(jnp.float32) * value.astype(jnp.float32)
    grad_z = cotangent.astype(jnp.float32) * query.astype(jnp.float32)
    spread = jnp.sqrt((1.0 - decay) * (1.0 + decay))
    coeffs = residue * spread
    zero_state = jnp.zeros(decay.shape, jnp.float32)

    def forward(carry, inputs):
        state, total = carry
        inner_row, grad_row = inputs
        state = decay * state + inner_row[None, :]
        total = total + grad_row[None, :] * state
        return ((state, total), lax.optimization_barrier(jnp.sum(coeffs * state, axis=0)))
    (last_state, totals), mixed = lax.scan(forward, (zero_state, zero_state), (inner, grad_z))
    mixed_z = mixed + skip[None, :] * inner

    def backward(state, grad_row):
        state = decay * state + grad_row[None, :]
        return (state, lax.optimization_barrier(jnp.sum(coeffs * state, axis=0)))
    first_state, back_mixed = lax.scan(backward, zero_state, grad_z, reverse=True)
    inner_grad = back_mixed + skip[None, :] * grad_z
    scale = 1.0 / math.sqrt(SEQ)
    output = (query.astype(jnp.float32) * mixed_z).astype(jnp.bfloat16)
    query_grad = (cotangent.astype(jnp.float32) * mixed_z).astype(jnp.bfloat16)
    key_grad = (inner_grad * value.astype(jnp.float32)).astype(jnp.bfloat16)
    value_grad = (inner_grad * key.astype(jnp.float32)).astype(jnp.bfloat16)
    residue_grad = spread * totals * scale
    skip_grad = lax.optimization_barrier(jnp.sum(grad_z * inner, axis=0)) * scale
    return (output, query_grad, key_grad, value_grad, residue_grad, skip_grad)
```

```python
import functools
import math

import jax
import jax.numpy as jnp
from jax import lax
from jax.experimental import pallas as pl
from jax.experimental.pallas import tpu as pltpu
from jax.sharding import PartitionSpec as P

LANES = 128
SEGS = 8
F32 = jnp.float32
MESH = pl.DeviceIdType.MESH


def each(low, high, body):
    if high - low <= 16:
        for step in range(low, high):
            body(step)
    else:
        def wrapped(step, carry):
            body(step)
            return carry

        lax.fori_loop(low, high, wrapped, 0)


def power(base, exponent):
    result = None
    while exponent:
        if exponent & 1:
            result = base if result is None else result * base
        exponent >>= 1
        if exponent:
            base = base * base
    return result


def kernel(
    n, m, scale,
    q_hbm, k_hbm, v_hbm, g_hbm, decay_hbm, residue_hbm, skip_hbm,
    out_hbm, dq_hbm, dk_hbm, dv_hbm, res_ref, skipg_ref,
    q_in, k_in, v_in, g_in, decay, residue, skip, coef,
    out_v, dq_v, dk_v, dv_v,
    x_s, z_s, y_s, u_s, seg, start,
    mine, gath, ret, carry, rsend, rgath, rtot,
    in_sem, par_sem, out_sem, s1s, s1r, s2s, s2r, s3s, s3r, s4s, s4r,
):
    me = lax.axis_index("ctx")
    rows = q_hbm.shape[0]
    width = q_hbm.shape[1] // m
    tiles = width // LANES
    modes = decay_hbm.shape[0]
    steps = rows // SEGS
    stride = n // m
    own = me // stride
    hbm_in = (q_hbm, k_hbm, v_hbm, g_hbm)
    vmem_in = (q_in, k_in, v_in, g_in)
    hbm_out = (out_hbm, dq_hbm, dk_hbm, dv_hbm)
    vmem_out = (out_v, dq_v, dk_v, dv_v)

    def block_of(step):
        return lax.rem(me + 1 + step, m)

    def lanes_of(block, tile=None):
        if tile is None:
            return pl.ds(pl.multiple_of(block * width, LANES), width)
        return pl.ds(pl.multiple_of(block * width + tile * LANES, LANES), LANES)

    def load_copy(index, block):
        return pltpu.make_async_copy(
            hbm_in[index].at[:, lanes_of(block)], vmem_in[index].at[block],
            in_sem.at[index, block],
        )

    def store_copy(index, block):
        return pltpu.make_async_copy(
            vmem_out[index].at[block], hbm_out[index].at[:, lanes_of(block)],
            out_sem.at[index, block],
        )

    params = [
        pltpu.make_async_copy(decay_hbm, decay, par_sem.at[0]),
        pltpu.make_async_copy(residue_hbm, residue, par_sem.at[1]),
        pltpu.make_async_copy(skip_hbm, skip, par_sem.at[2]),
    ]

    def remote(src, dst, send_sem, recv_sem, device):
        return pltpu.make_async_remote_copy(
            src_ref=src, dst_ref=dst, send_sem=send_sem, recv_sem=recv_sem,
            device_id={"ctx": device}, device_id_type=MESH,
        )

    def ends_copy(block):
        return remote(mine.at[block], gath.at[me], s1s.at[block], s1r.at[me], block * stride)

    def return_copy(peer):
        return remote(ret.at[peer], carry.at[own], s2s.at[peer], s2r.at[own], peer)

    def sums_copy(block):
        return remote(rsend.at[block], rgath.at[me], s3s.at[block], s3r.at[me], block * stride)

    def total_copy(peer):
        return remote(rtot.at[own], rtot.at[own], s4s.at[peer], s4r.at[own], peer)

    def as_owner(body):
        if stride == 1:
            body()
        else:
            pl.when(lax.rem(me, stride) == 0)(body)

    def peers(body):
        each(1, n, lambda r: body(lax.rem(me + r, n)))

    def row(ref, mode, block, tile):
        return jnp.broadcast_to(ref[mode:mode + 1, lanes_of(block, tile)], (SEGS, LANES))

    def strided(index):
        return pl.ds(index, SEGS, stride=steps)

    barrier = pltpu.get_barrier_semaphore()
    for copy in params:
        copy.start()
    for step in range(m):
        for index in range(4):
            load_copy(index, block_of(step)).start()
    peers(lambda peer: pl.semaphore_signal(
        barrier, inc=1, device_id={"ctx": peer}, device_id_type=MESH))
    for copy in params:
        copy.wait()

    def first_pass(block):
        for index in range(4):
            load_copy(index, block).wait()
        for tile in range(tiles):
            spot = block * tiles + tile
            here = slice(tile * LANES, (tile + 1) * LANES)
            x_s[spot] = k_in[block, :, here].astype(F32) * v_in[block, :, here].astype(F32)
            z_s[spot] = g_in[block, :, here].astype(F32) * q_in[block, :, here].astype(F32)
            d_all = decay[:, lanes_of(block, tile)]
            spread = jnp.sqrt((1.0 - d_all) * (1.0 + d_all))
            coef[:, lanes_of(block, tile)] = residue[:, lanes_of(block, tile)] * spread
            d = [row(decay, mode, block, tile) for mode in range(modes)]
            tail = [None] * modes
            head = [None] * modes
            for i in range(steps):
                x = x_s[spot, strided(i), :]
                z = z_s[spot, strided(steps - 1 - i), :]
                for mode in range(modes):
                    tail[mode] = x if i == 0 else d[mode] * tail[mode] + x
                    head[mode] = z if i == 0 else d[mode] * head[mode] + z
            for mode in range(modes):
                seg[tile, mode * SEGS:(mode + 1) * SEGS, :] = tail[mode]
                seg[tile, (modes + mode) * SEGS:(modes + mode + 1) * SEGS, :] = head[mode]
            d_seg = power(d_all, steps)
            total = jnp.zeros((modes, LANES), F32)
            for j in range(SEGS):
                at = pl.ds(j, modes, stride=SEGS)
                start[spot, at, :] = total
                total = d_seg * total + seg[tile, at, :]
            mine[block, 0:modes, here] = total
            total = jnp.zeros((modes, LANES), F32)
            for j in reversed(range(SEGS)):
                at = pl.ds(modes * SEGS + j, modes, stride=SEGS)
                start[spot, at, :] = total
                total = d_seg * total + seg[tile, at, :]
            mine[block, modes:2 * modes, here] = total

    def send_ends(block):
        @pl.when(block * stride != me)
        def _():
            ends_copy(block).start()

        @pl.when(block * stride == me)
        def _():
            gath[me] = mine[block]

    def middle_pass(block):
        for tile in range(tiles):
            spot = block * tiles + tile
            here = slice(tile * LANES, (tile + 1) * LANES)
            d = [row(decay, mode, block, tile) for mode in range(modes)]
            c = [row(coef, mode, block, tile) for mode in range(modes)]
            sk = row(skip, 0, block, tile)
            state = [start[spot, mode * SEGS:(mode + 1) * SEGS, :] for mode in range(modes)]
            back = [
                start[spot, (modes + mode) * SEGS:(modes + mode + 1) * SEGS, :]
                for mode in range(modes)
            ]
            sums = [jnp.zeros((SEGS, LANES), F32) for _ in range(modes + 1)]
            for i in range(steps):
                x = x_s[spot, strided(i), :]
                z = z_s[spot, strided(i), :]
                y = sk * x
                sums[modes] = sums[modes] + z * x
                for mode in range(modes):
                    state[mode] = d[mode] * state[mode] + x
                    y = y + c[mode] * state[mode]
                    sums[mode] = sums[mode] + z * state[mode]
                y_s[spot, strided(i), :] = y
                z = z_s[spot, strided(steps - 1 - i), :]
                u = sk * z
                for mode in range(modes):
                    back[mode] = d[mode] * back[mode] + z
                    u = u + c[mode] * back[mode]
                u_s[spot, strided(steps - 1 - i), :] = u
            for mode in range(modes + 1):
                rsend[block, mode:mode + 1, here] = jnp.sum(sums[mode], axis=0, keepdims=True)
            rsend[block, modes + 1:, here] = jnp.zeros((2 * modes - modes - 1, LANES), F32)

    def send_sums(block):
        @pl.when(block * stride != me)
        def _():
            sums_copy(block).start()

        @pl.when(block * stride == me)
        def _():
            rgath[me] = rsend[block]

    def owner_scan():
        peers(lambda peer: remote(
            gath.at[peer], gath.at[peer], s1s.at[0], s1r.at[peer], peer).wait_recv())
        d_rows = power(decay[:, lanes_of(own)], rows)

        def forward(p, total):
            ret[p, 0:modes, :] = total
            return d_rows * total + gath[p, 0:modes, :]

        def backward(p, total):
            ret[n - 1 - p, modes:2 * modes, :] = total
            return d_rows * total + gath[n - 1 - p, modes:2 * modes, :]

        zero = jnp.zeros((modes, width), F32)
        lax.fori_loop(0, n, forward, zero, unroll=n <= 16)
        lax.fori_loop(0, n, backward, zero, unroll=n <= 16)
        carry[own] = ret[me]
        peers(lambda peer: return_copy(peer).start())

    def owner_sums():
        peers(lambda peer: remote(
            rgath.at[peer], rgath.at[peer], s3s.at[0], s3r.at[peer], peer).wait_recv())

        def add(p, total):
            return (
                total[0] + rgath[p],
                total[1] + gath[p, modes:2 * modes, :] * ret[p, 0:modes, :],
            )

        whole, cross = lax.fori_loop(
            0, n, add,
            (jnp.zeros((2 * modes, width), F32), jnp.zeros((modes, width), F32)),
            unroll=n <= 16,
        )
        d_all = decay[:, lanes_of(own)]
        spread = jnp.sqrt((1.0 - d_all) * (1.0 + d_all))
        rtot[own, 0:modes, :] = (whole[0:modes] + d_all * cross) * (spread * scale)
        rtot[own, modes:2 * modes, :] = whole[modes:2 * modes] * scale
        peers(lambda peer: total_copy(peer).start())

    place = lax.broadcasted_iota(jnp.int32, (SEGS, LANES), 0)
    bits = [(place & (1 << bit)) != 0 for bit in range(3)]

    def last_pass(block):
        for tile in range(tiles):
            spot = block * tiles + tile
            here = slice(tile * LANES, (tile + 1) * LANES)
            fall = []
            fore = []
            aft = []
            for mode in range(modes):
                base = row(decay, mode, block, tile)
                weight = row(coef, mode, block, tile) * base
                up = weight * jnp.broadcast_to(carry[block, mode:mode + 1, here], (SEGS, LANES))
                down = weight * jnp.broadcast_to(
                    carry[block, modes + mode:modes + mode + 1, here], (SEGS, LANES))
                for bit in bits:
                    up = jnp.where(bit, up * base, up)
                    down = jnp.where(bit, down, down * base)
                    base = base * base
                fall.append(base)
                fore.append(up)
                aft.append(down)
            for pair in range(rows // 16):
                parts = []
                for half in range(2):
                    at = slice(pair * 16 + half * 8, pair * 16 + half * 8 + 8)
                    parts.append(y_s[spot, at, :] + ((fore[0] + fore[1]) + (fore[2] + fore[3])))
                    fore = [value * rate for value, rate in zip(fore, fall)]
                mixed = jnp.concatenate(parts, axis=0)
                at = slice(pair * 16, pair * 16 + 16)
                out_v[block, at, here] = (q_in[block, at, here].astype(F32) * mixed).astype(jnp.bfloat16)
                dq_v[block, at, here] = (g_in[block, at, here].astype(F32) * mixed).astype(jnp.bfloat16)
                pair = rows // 16 - 1 - pair
                parts = []
                for half in (1, 0):
                    at = slice(pair * 16 + half * 8, pair * 16 + half * 8 + 8)
                    parts.append(u_s[spot, at, :] + ((aft[0] + aft[1]) + (aft[2] + aft[3])))
                    aft = [value * rate for value, rate in zip(aft, fall)]
                mixed = jnp.concatenate(parts[::-1], axis=0)
                at = slice(pair * 16, pair * 16 + 16)
                dk_v[block, at, here] = (v_in[block, at, here].astype(F32) * mixed).astype(jnp.bfloat16)
                dv_v[block, at, here] = (k_in[block, at, here].astype(F32) * mixed).astype(jnp.bfloat16)

    first_pass(block_of(0))
    pl.semaphore_wait(barrier, n - 1)
    send_ends(block_of(0))

    @pl.loop(1, m)
    def _(step):
        block = block_of(step)
        first_pass(block)
        send_ends(block)

    half = m // 2

    def middle(step):
        block = block_of(step)
        middle_pass(block)
        send_sums(block)

    pl.loop(0, half)(middle)
    as_owner(owner_scan)
    pl.loop(half, m)(middle)

    def last(step):
        block = block_of(m - 1 + step)

        @pl.when(block * stride != me)
        def _():
            remote(carry.at[block], carry.at[block], s2s.at[0], s2r.at[block], me).wait_recv()

        last_pass(block)
        for index in range(4):
            store_copy(index, block).start()

    pl.loop(0, half)(last)
    as_owner(owner_sums)
    pl.loop(half, m)(last)

    for block in range(m):
        @pl.when(block * stride != me)
        def _():
            remote(rtot.at[block], rtot.at[block], s4s.at[0], s4r.at[block], me).wait_recv()
            ends_copy(block).wait_send()
            sums_copy(block).wait_send()

        at = slice(block * width, (block + 1) * width)
        res_ref[:, at] = rtot[block, 0:modes, :]
        skipg_ref[:, at] = rtot[block, modes:modes + 1, :]

    def sent():
        def one(peer):
            return_copy(peer).wait_send()
            total_copy(peer).wait_send()

        peers(one)

    as_owner(sent)

    @pl.loop(0, m)
    def _(block):
        for index in range(4):
            store_copy(index, block).wait()


def local(n, query, key, value, cotangent, decay, residue, skip):
    rows, chans = query.shape
    modes = decay.shape[0]
    m = min(n, chans // LANES)
    width = chans // m
    scale = 1.0 / math.sqrt(rows * n)
    wide = jax.ShapeDtypeStruct((rows, chans), jnp.bfloat16)
    anywhere = pl.BlockSpec(memory_space=pl.ANY)
    vmem = pl.BlockSpec(memory_space=pltpu.VMEM)
    blocks16 = pltpu.VMEM((m, rows, width), jnp.bfloat16)
    plane = pltpu.VMEM((chans // LANES, rows, LANES), F32)
    by_owner = pltpu.VMEM((m, 2 * modes, width), F32)
    by_device = pltpu.VMEM((n, 2 * modes, width), F32)
    dma = pltpu.SemaphoreType.DMA
    outs = pl.pallas_call(
        functools.partial(kernel, n, m, scale),
        out_shape=(
            wide, wide, wide, wide,
            jax.ShapeDtypeStruct((modes, chans), F32),
            jax.ShapeDtypeStruct((1, chans), F32),
        ),
        in_specs=[anywhere] * 7,
        out_specs=(anywhere,) * 4 + (vmem,) * 2,
        scratch_shapes=[
            blocks16, blocks16, blocks16, blocks16,
            pltpu.VMEM((modes, chans), F32),
            pltpu.VMEM((modes, chans), F32),
            pltpu.VMEM((1, chans), F32),
            pltpu.VMEM((modes, chans), F32),
            blocks16, blocks16, blocks16, blocks16,
            plane, plane, plane, plane,
            pltpu.VMEM((width // LANES, 2 * modes * SEGS, LANES), F32),
            pltpu.VMEM((chans // LANES, 2 * modes * SEGS, LANES), F32),
            by_owner, by_device, by_device, by_owner, by_owner, by_device, by_owner,
            dma((4, m)), dma((3,)), dma((4, m)),
            dma((m,)), dma((n,)), dma((n,)), dma((m,)),
            dma((m,)), dma((n,)), dma((n,)), dma((m,)),
        ],
        compiler_params=pltpu.CompilerParams(
            collective_id=0, has_side_effects=True, vmem_limit_bytes=20 * 1024 * 1024,
        ),
        cost_estimate=pl.CostEstimate(
            flops=80 * rows * chans, bytes_accessed=16 * rows * chans, transcendentals=0
        ),
        name="hyena",
    )(query, key, value, cotangent, decay, residue, skip.reshape(1, chans))
    return outs[:5] + (outs[5].reshape(chans),)


def solution(mesh):
    wide = P("ctx", "ch")
    thin = P(None, "ch")
    return jax.shard_map(
        functools.partial(local, mesh.shape["ctx"]),
        mesh=mesh,
        in_specs=(wide, wide, wide, wide, thin, thin, P("ch")),
        out_specs=(wide, wide, wide, wide, thin, P("ch")),
        check_vma=False,
    )
```

```python
import functools
import math

import jax
import jax.numpy as jnp
from jax import lax
from jax.experimental import pallas as pl
from jax.experimental.pallas import tpu as pltpu
from jax.sharding import PartitionSpec as P

LANES = 128
SEGS = 8
F32 = jnp.float32
MESH = pl.DeviceIdType.MESH


def each(low, high, body):
    if high - low <= 16:
        for step in range(low, high):
            body(step)
    else:
        def wrapped(step, carry):
            body(step)
            return carry

        lax.fori_loop(low, high, wrapped, 0)


def power(base, exponent):
    result = None
    while exponent:
        if exponent & 1:
            result = base if result is None else result * base
        exponent >>= 1
        if exponent:
            base = base * base
    return result


def kernel(
    n, m, scale,
    q_hbm, k_hbm, v_hbm, g_hbm, decay_hbm, residue_hbm, skip_hbm,
    out_v, dq_v, dk_v, dv_v, res_ref, skipg_ref,
    q_in, k_in, v_in, g_in, decay, residue, skip, coef,
    x_s, z_s, y_s, u_s, seg, start,
    mine, gath, ret, carry, rsend, rgath, rtot,
    in_sem, par_sem, s1s, s1r, s2s, s2r, s3s, s3r, s4s, s4r,
):
    me = lax.axis_index("ctx")
    rows = q_hbm.shape[0]
    width = q_hbm.shape[1] // m
    tiles = width // LANES
    modes = decay_hbm.shape[0]
    steps = rows // SEGS
    stride = n // m
    own = me // stride
    hbm_in = (q_hbm, k_hbm, v_hbm, g_hbm)
    vmem_in = (q_in, k_in, v_in, g_in)

    def block_of(step):
        return lax.rem(me + 1 + step, m)

    def lanes_of(block, tile=None):
        if tile is None:
            return pl.ds(pl.multiple_of(block * width, LANES), width)
        return pl.ds(pl.multiple_of(block * width + tile * LANES, LANES), LANES)

    def load_copy(index, block):
        return pltpu.make_async_copy(
            hbm_in[index].at[:, lanes_of(block)], vmem_in[index].at[block],
            in_sem.at[index, block],
        )

    params = [
        pltpu.make_async_copy(decay_hbm, decay, par_sem.at[0]),
        pltpu.make_async_copy(residue_hbm, residue, par_sem.at[1]),
        pltpu.make_async_copy(skip_hbm, skip, par_sem.at[2]),
    ]

    def remote(src, dst, send_sem, recv_sem, device):
        return pltpu.make_async_remote_copy(
            src_ref=src, dst_ref=dst, send_sem=send_sem, recv_sem=recv_sem,
            device_id={"ctx": device}, device_id_type=MESH,
        )

    def ends_copy(block):
        return remote(mine.at[block], gath.at[me], s1s.at[block], s1r.at[me], block * stride)

    def return_copy(peer):
        return remote(ret.at[peer], carry.at[own], s2s.at[peer], s2r.at[own], peer)

    def sums_copy(block):
        return remote(rsend.at[block], rgath.at[me], s3s.at[block], s3r.at[me], block * stride)

    def total_copy(peer):
        return remote(rtot.at[own], rtot.at[own], s4s.at[peer], s4r.at[own], peer)

    def as_owner(body):
        if stride == 1:
            body()
        else:
            pl.when(lax.rem(me, stride) == 0)(body)

    def peers(body):
        each(1, n, lambda r: body(lax.rem(me + r, n)))

    def row(ref, mode, block, tile):
        return jnp.broadcast_to(ref[mode:mode + 1, lanes_of(block, tile)], (SEGS, LANES))

    def strided(index):
        return pl.ds(index, SEGS, stride=steps + 1)

    def padded(first, count):
        return pl.ds(first + first // steps, count)

    barrier = pltpu.get_barrier_semaphore()
    for copy in params:
        copy.start()
    for step in range(m):
        for index in range(4):
            load_copy(index, block_of(step)).start()
    peers(lambda peer: pl.semaphore_signal(
        barrier, inc=1, device_id={"ctx": peer}, device_id_type=MESH))
    for copy in params:
        copy.wait()

    def first_pass(block):
        for index in range(4):
            load_copy(index, block).wait()
        for tile in range(tiles):
            spot = block * tiles + tile
            here = slice(tile * LANES, (tile + 1) * LANES)
            for j in range(SEGS):
                at = slice(j * steps, (j + 1) * steps)
                to = padded(j * steps, steps)
                x_s[spot, to, :] = k_in[block, at, here].astype(F32) * v_in[block, at, here].astype(F32)
                z_s[spot, to, :] = g_in[block, at, here].astype(F32) * q_in[block, at, here].astype(F32)
            d_all = decay[:, lanes_of(block, tile)]
            spread = jnp.sqrt((1.0 - d_all) * (1.0 + d_all))
            coef[:, lanes_of(block, tile)] = residue[:, lanes_of(block, tile)] * spread
            d = [row(decay, mode, block, tile) for mode in range(modes)]
            tail = [None] * modes
            head = [None] * modes
            for i in range(steps):
                x = x_s[spot, strided(i), :]
                z = z_s[spot, strided(steps - 1 - i), :]
                for mode in range(modes):
                    tail[mode] = x if i == 0 else d[mode] * tail[mode] + x
                    head[mode] = z if i == 0 else d[mode] * head[mode] + z
            for mode in range(modes):
                seg[tile, mode * SEGS:(mode + 1) * SEGS, :] = tail[mode]
                seg[tile, (modes + mode) * SEGS:(modes + mode + 1) * SEGS, :] = head[mode]
            d_seg = power(d_all, steps)
            total = jnp.zeros((modes, LANES), F32)
            for j in range(SEGS):
                at = pl.ds(j, modes, stride=SEGS)
                start[spot, at, :] = total
                total = d_seg * total + seg[tile, at, :]
            mine[block, 0:modes, here] = total
            total = jnp.zeros((modes, LANES), F32)
            for j in reversed(range(SEGS)):
                at = pl.ds(modes * SEGS + j, modes, stride=SEGS)
                start[spot, at, :] = total
                total = d_seg * total + seg[tile, at, :]
            mine[block, modes:2 * modes, here] = total

    def send_ends(block):
        @pl.when(block * stride != me)
        def _():
            ends_copy(block).start()

        @pl.when(block * stride == me)
        def _():
            gath[me] = mine[block]

    def middle_pass(block):
        for tile in range(tiles):
            spot = block * tiles + tile
            here = slice(tile * LANES, (tile + 1) * LANES)
            d = [row(decay, mode, block, tile) for mode in range(modes)]
            c = [row(coef, mode, block, tile) for mode in range(modes)]
            sk = row(skip, 0, block, tile)
            state = [start[spot, mode * SEGS:(mode + 1) * SEGS, :] for mode in range(modes)]
            back = [
                start[spot, (modes + mode) * SEGS:(modes + mode + 1) * SEGS, :]
                for mode in range(modes)
            ]
            sums = [jnp.zeros((SEGS, LANES), F32) for _ in range(modes + 1)]
            for i in range(steps):
                x = x_s[spot, strided(i), :]
                z = z_s[spot, strided(i), :]
                y = sk * x
                sums[modes] = sums[modes] + z * x
                for mode in range(modes):
                    state[mode] = d[mode] * state[mode] + x
                    y = y + c[mode] * state[mode]
                    sums[mode] = sums[mode] + z * state[mode]
                y_s[spot, strided(i), :] = y
                z = z_s[spot, strided(steps - 1 - i), :]
                u = sk * z
                for mode in range(modes):
                    back[mode] = d[mode] * back[mode] + z
                    u = u + c[mode] * back[mode]
                u_s[spot, strided(steps - 1 - i), :] = u
            for mode in range(modes + 1):
                rsend[block, mode:mode + 1, here] = jnp.sum(sums[mode], axis=0, keepdims=True)
            rsend[block, modes + 1:, here] = jnp.zeros((2 * modes - modes - 1, LANES), F32)

    def send_sums(block):
        @pl.when(block * stride != me)
        def _():
            sums_copy(block).start()

        @pl.when(block * stride == me)
        def _():
            rgath[me] = rsend[block]

    def owner_scan():
        peers(lambda peer: remote(
            gath.at[peer], gath.at[peer], s1s.at[0], s1r.at[peer], peer).wait_recv())
        d_rows = power(decay[:, lanes_of(own)], rows)

        def forward(p, total):
            ret[p, 0:modes, :] = total
            return d_rows * total + gath[p, 0:modes, :]

        def backward(p, total):
            ret[n - 1 - p, modes:2 * modes, :] = total
            return d_rows * total + gath[n - 1 - p, modes:2 * modes, :]

        zero = jnp.zeros((modes, width), F32)
        lax.fori_loop(0, n, forward, zero, unroll=n <= 16)
        lax.fori_loop(0, n, backward, zero, unroll=n <= 16)
        carry[own] = ret[me]
        peers(lambda peer: return_copy(peer).start())

    def owner_sums():
        peers(lambda peer: remote(
            rgath.at[peer], rgath.at[peer], s3s.at[0], s3r.at[peer], peer).wait_recv())

        def add(p, total):
            return (
                total[0] + rgath[p],
                total[1] + gath[p, modes:2 * modes, :] * ret[p, 0:modes, :],
            )

        whole, cross = lax.fori_loop(
            0, n, add,
            (jnp.zeros((2 * modes, width), F32), jnp.zeros((modes, width), F32)),
            unroll=n <= 16,
        )
        d_all = decay[:, lanes_of(own)]
        spread = jnp.sqrt((1.0 - d_all) * (1.0 + d_all))
        rtot[own, 0:modes, :] = (whole[0:modes] + d_all * cross) * (spread * scale)
        rtot[own, modes:2 * modes, :] = whole[modes:2 * modes] * scale
        peers(lambda peer: total_copy(peer).start())

    place = lax.broadcasted_iota(jnp.int32, (SEGS, LANES), 0)
    bits = [(place & (1 << bit)) != 0 for bit in range(3)]

    def last_pass(block):
        for tile in range(tiles):
            spot = block * tiles + tile
            here = slice(tile * LANES, (tile + 1) * LANES)
            fall = []
            fore = []
            aft = []
            for mode in range(modes):
                base = row(decay, mode, block, tile)
                weight = row(coef, mode, block, tile) * base
                up = weight * jnp.broadcast_to(carry[block, mode:mode + 1, here], (SEGS, LANES))
                down = weight * jnp.broadcast_to(
                    carry[block, modes + mode:modes + mode + 1, here], (SEGS, LANES))
                for bit in bits:
                    up = jnp.where(bit, up * base, up)
                    down = jnp.where(bit, down, down * base)
                    base = base * base
                fall.append(base)
                fore.append(up)
                aft.append(down)
            for pair in range(rows // 16):
                parts = []
                for half in range(2):
                    at = padded(pair * 16 + half * 8, 8)
                    parts.append(y_s[spot, at, :] + ((fore[0] + fore[1]) + (fore[2] + fore[3])))
                    fore = [value * rate for value, rate in zip(fore, fall)]
                mixed = jnp.concatenate(parts, axis=0)
                at = slice(pair * 16, pair * 16 + 16)
                out_v[block, at, here] = (q_in[block, at, here].astype(F32) * mixed).astype(jnp.bfloat16)
                dq_v[block, at, here] = (g_in[block, at, here].astype(F32) * mixed).astype(jnp.bfloat16)
                pair = rows // 16 - 1 - pair
                parts = []
                for half in (1, 0):
                    at = padded(pair * 16 + half * 8, 8)
                    parts.append(u_s[spot, at, :] + ((aft[0] + aft[1]) + (aft[2] + aft[3])))
                    aft = [value * rate for value, rate in zip(aft, fall)]
                mixed = jnp.concatenate(parts[::-1], axis=0)
                at = slice(pair * 16, pair * 16 + 16)
                dk_v[block, at, here] = (v_in[block, at, here].astype(F32) * mixed).astype(jnp.bfloat16)
                dv_v[block, at, here] = (k_in[block, at, here].astype(F32) * mixed).astype(jnp.bfloat16)

    first_pass(block_of(0))
    pl.semaphore_wait(barrier, n - 1)
    send_ends(block_of(0))

    @pl.loop(1, m)
    def _(step):
        block = block_of(step)
        first_pass(block)
        send_ends(block)

    half = m // 2

    def middle(step):
        block = block_of(step)
        middle_pass(block)
        send_sums(block)

    pl.loop(0, half)(middle)
    as_owner(owner_scan)
    pl.loop(half, m)(middle)

    def last(step):
        block = block_of(m - 1 + step)

        @pl.when(block * stride != me)
        def _():
            remote(carry.at[block], carry.at[block], s2s.at[0], s2r.at[block], me).wait_recv()

        last_pass(block)

    pl.loop(0, half)(last)
    as_owner(owner_sums)
    pl.loop(half, m)(last)

    for block in range(m):
        @pl.when(block * stride != me)
        def _():
            remote(rtot.at[block], rtot.at[block], s4s.at[0], s4r.at[block], me).wait_recv()
            ends_copy(block).wait_send()
            sums_copy(block).wait_send()

        at = slice(block * width, (block + 1) * width)
        res_ref[:, at] = rtot[block, 0:modes, :]
        skipg_ref[:, at] = rtot[block, modes:modes + 1, :]

    def sent():
        def one(peer):
            return_copy(peer).wait_send()
            total_copy(peer).wait_send()

        peers(one)

    as_owner(sent)


def write_kernel(m, *refs):
    sem = refs[12]
    width = refs[6].shape[1] // m
    copies = []
    for index in range(4):
        for block in range(m):
            copies.append(pltpu.make_async_copy(
                refs[index].at[block],
                refs[6 + index].at[:, block * width:(block + 1) * width],
                sem.at[index, block],
            ))
    for index in range(4, 6):
        copies.append(pltpu.make_async_copy(refs[index], refs[6 + index], sem.at[index, 0]))
    for copy in copies:
        copy.start()
    for copy in copies:
        copy.wait()


def local(n, query, key, value, cotangent, decay, residue, skip):
    rows, chans = query.shape
    modes = decay.shape[0]
    m = min(n, chans // LANES)
    width = chans // m
    scale = 1.0 / math.sqrt(rows * n)
    wide = jax.ShapeDtypeStruct((rows, chans), jnp.bfloat16)
    blocked = jax.ShapeDtypeStruct((m, rows, width), jnp.bfloat16)
    small = (
        jax.ShapeDtypeStruct((modes, chans), F32), jax.ShapeDtypeStruct((1, chans), F32),
    )
    hbm = pl.BlockSpec(memory_space=pltpu.HBM)
    vmem = pl.BlockSpec(memory_space=pltpu.VMEM)
    blocks16 = pltpu.VMEM((m, rows, width), jnp.bfloat16)
    plane = pltpu.VMEM((chans // LANES, rows + SEGS, LANES), F32)
    by_owner = pltpu.VMEM((m, 2 * modes, width), F32)
    by_device = pltpu.VMEM((n, 2 * modes, width), F32)
    dma = pltpu.SemaphoreType.DMA
    outs = pl.pallas_call(
        functools.partial(kernel, n, m, scale),
        out_shape=(blocked,) * 4 + small,
        in_specs=[hbm] * 7,
        out_specs=(vmem,) * 6,
        scratch_shapes=[
            blocks16, blocks16, blocks16, blocks16,
            pltpu.VMEM((modes, chans), F32),
            pltpu.VMEM((modes, chans), F32),
            pltpu.VMEM((1, chans), F32),
            pltpu.VMEM((modes, chans), F32),
            plane, plane, plane, plane,
            pltpu.VMEM((width // LANES, 2 * modes * SEGS, LANES), F32),
            pltpu.VMEM((chans // LANES, 2 * modes * SEGS, LANES), F32),
            by_owner, by_device, by_device, by_owner, by_owner, by_device, by_owner,
            dma((4, m)), dma((3,)),
            dma((m,)), dma((n,)), dma((n,)), dma((m,)),
            dma((m,)), dma((n,)), dma((n,)), dma((m,)),
        ],
        compiler_params=pltpu.CompilerParams(
            collective_id=0, has_side_effects=True, vmem_limit_bytes=20 * 1024 * 1024,
        ),
        cost_estimate=pl.CostEstimate(
            flops=80 * rows * chans, bytes_accessed=16 * rows * chans, transcendentals=0
        ),
        name="hyena",
    )(*[
        pltpu.with_memory_space_constraint(array, pltpu.HBM)
        for array in (query, key, value, cotangent, decay, residue, skip.reshape(1, chans))
    ])
    outs = pl.pallas_call(
        functools.partial(write_kernel, m),
        out_shape=(wide,) * 4 + small,
        in_specs=[vmem] * 6,
        out_specs=(hbm,) * 6,
        scratch_shapes=[dma((6, m))],
        cost_estimate=pl.CostEstimate(
            flops=0, bytes_accessed=16 * rows * chans, transcendentals=0
        ),
        name="write",
    )(*outs)
    return outs[:5] + (outs[5].reshape(chans),)


def solution(mesh):
    wide = P("ctx", "ch")
    thin = P(None, "ch")
    return jax.shard_map(
        functools.partial(local, mesh.shape["ctx"]),
        mesh=mesh,
        in_specs=(wide, wide, wide, wide, thin, thin, P("ch")),
        out_specs=(wide, wide, wide, wide, thin, P("ch")),
        check_vma=False,
    )
```

```python
import functools
import math

import jax
import jax.numpy as jnp
from jax import lax
from jax.experimental import pallas as pl
from jax.experimental.pallas import tpu as pltpu
from jax.sharding import PartitionSpec as P

LANES = 128
SEGS = 8
F32 = jnp.float32
MESH = pl.DeviceIdType.MESH


def each(low, high, body):
    if high - low <= 16:
        for step in range(low, high):
            body(step)
    else:
        def wrapped(step, carry):
            body(step)
            return carry

        lax.fori_loop(low, high, wrapped, 0)


def power(base, exponent):
    result = None
    while exponent:
        if exponent & 1:
            result = base if result is None else result * base
        exponent >>= 1
        if exponent:
            base = base * base
    return result


def kernel(
    n, m, scale,
    q_hbm, k_hbm, v_hbm, g_hbm, decay_hbm, residue_hbm, skip_hbm,
    q_in, k_in, v_in, g_in, y_s, u_s, decay, coef, carried, res_ref, skipg_ref,
    residue, skip, x_s, z_s, seg, start,
    mine, gath, ret, carry, rsend, rgath, rtot,
    in_sem, par_sem, s1s, s1r, s2s, s2r, s3s, s3r, s4s, s4r,
):
    me = lax.axis_index("ctx")
    rows = q_hbm.shape[0]
    width = q_hbm.shape[1] // m
    tiles = width // LANES
    modes = decay_hbm.shape[0]
    steps = rows // SEGS
    stride = n // m
    own = me // stride
    hbm_in = (q_hbm, k_hbm, v_hbm, g_hbm)
    vmem_in = (q_in, k_in, v_in, g_in)

    def block_of(step):
        return lax.rem(me + 1 + step, m)

    def lanes_of(block, tile=None):
        if tile is None:
            return pl.ds(pl.multiple_of(block * width, LANES), width)
        return pl.ds(pl.multiple_of(block * width + tile * LANES, LANES), LANES)

    def load_copy(index, block):
        return pltpu.make_async_copy(
            hbm_in[index].at[:, lanes_of(block)], vmem_in[index].at[block],
            in_sem.at[index, block],
        )

    params = [
        pltpu.make_async_copy(decay_hbm, decay, par_sem.at[0]),
        pltpu.make_async_copy(residue_hbm, residue, par_sem.at[1]),
        pltpu.make_async_copy(skip_hbm, skip, par_sem.at[2]),
    ]

    def remote(src, dst, send_sem, recv_sem, device):
        return pltpu.make_async_remote_copy(
            src_ref=src, dst_ref=dst, send_sem=send_sem, recv_sem=recv_sem,
            device_id={"ctx": device}, device_id_type=MESH,
        )

    def ends_copy(block):
        return remote(mine.at[block], gath.at[me], s1s.at[block], s1r.at[me], block * stride)

    def return_copy(peer):
        return remote(ret.at[peer], carry.at[own], s2s.at[peer], s2r.at[own], peer)

    def sums_copy(block):
        return remote(rsend.at[block], rgath.at[me], s3s.at[block], s3r.at[me], block * stride)

    def total_copy(peer):
        return remote(rtot.at[own], rtot.at[own], s4s.at[peer], s4r.at[own], peer)

    def as_owner(body):
        if stride == 1:
            body()
        else:
            pl.when(lax.rem(me, stride) == 0)(body)

    def peers(body):
        each(1, n, lambda r: body(lax.rem(me + r, n)))

    def row(ref, mode, block, tile):
        return jnp.broadcast_to(ref[mode:mode + 1, lanes_of(block, tile)], (SEGS, LANES))

    def strided(index):
        return pl.ds(index, SEGS, stride=steps + 1)

    def padded(first, count):
        return pl.ds(first + first // steps, count)

    barrier = pltpu.get_barrier_semaphore()
    for copy in params:
        copy.start()
    for step in range(m):
        for index in range(4):
            load_copy(index, block_of(step)).start()
    peers(lambda peer: pl.semaphore_signal(
        barrier, inc=1, device_id={"ctx": peer}, device_id_type=MESH))
    for copy in params:
        copy.wait()

    def first_pass(block):
        for index in range(4):
            load_copy(index, block).wait()
        d = []
        for tile in range(tiles):
            spot = block * tiles + tile
            here = slice(tile * LANES, (tile + 1) * LANES)
            for j in range(SEGS):
                at = slice(j * steps, (j + 1) * steps)
                to = padded(j * steps, steps)
                x_s[spot, to, :] = k_in[block, at, here].astype(F32) * v_in[block, at, here].astype(F32)
                z_s[spot, to, :] = g_in[block, at, here].astype(F32) * q_in[block, at, here].astype(F32)
            d.append([row(decay, mode, block, tile) for mode in range(modes)])
        tail = [[None] * modes for _ in range(tiles)]
        head = [[None] * modes for _ in range(tiles)]
        for i in range(steps):
            for tile in range(tiles):
                spot = block * tiles + tile
                x = x_s[spot, strided(i), :]
                z = z_s[spot, strided(steps - 1 - i), :]
                for mode in range(modes):
                    tail[tile][mode] = x if i == 0 else d[tile][mode] * tail[tile][mode] + x
                    head[tile][mode] = z if i == 0 else d[tile][mode] * head[tile][mode] + z
        for tile in range(tiles):
            for mode in range(modes):
                seg[tile, mode * SEGS:(mode + 1) * SEGS, :] = tail[tile][mode]
                seg[tile, (modes + mode) * SEGS:(modes + mode + 1) * SEGS, :] = head[tile][mode]
        for tile in range(tiles):
            spot = block * tiles + tile
            here = slice(tile * LANES, (tile + 1) * LANES)
            d_all = decay[:, lanes_of(block, tile)]
            spread = jnp.sqrt((1.0 - d_all) * (1.0 + d_all))
            coef[:, lanes_of(block, tile)] = residue[:, lanes_of(block, tile)] * spread
            d_seg = power(d_all, steps)
            up = jnp.zeros((modes, LANES), F32)
            down = jnp.zeros((modes, LANES), F32)
            for j in range(SEGS):
                at = pl.ds(j, modes, stride=SEGS)
                start[spot, at, :] = up
                up = d_seg * up + seg[tile, at, :]
                at = pl.ds(modes * SEGS + SEGS - 1 - j, modes, stride=SEGS)
                start[spot, at, :] = down
                down = d_seg * down + seg[tile, at, :]
            mine[block, 0:modes, here] = up
            mine[block, modes:2 * modes, here] = down

    def send_ends(block):
        @pl.when(block * stride != me)
        def _():
            ends_copy(block).start()

        @pl.when(block * stride == me)
        def _():
            gath[me] = mine[block]

    def rows_of(ref, block, count):
        return [[row(ref, mode, block, tile) for mode in range(count)] for tile in range(tiles)]

    def states_of(first, block):
        return [
            [
                start[block * tiles + tile, (first + mode) * SEGS:(first + mode + 1) * SEGS, :]
                for mode in range(modes)
            ]
            for tile in range(tiles)
        ]

    def forward_pass(block):
        d = rows_of(decay, block, modes)
        c = rows_of(coef, block, modes)
        sk = rows_of(skip, block, 1)
        state = states_of(0, block)
        sums = [[None] * (modes + 1) for _ in range(tiles)]
        for i in range(steps):
            for tile in range(tiles):
                spot = block * tiles + tile
                x = x_s[spot, strided(i), :]
                z = z_s[spot, strided(i), :]
                y = sk[tile][0] * x
                terms = []
                for mode in range(modes):
                    now = d[tile][mode] * state[tile][mode] + x
                    state[tile][mode] = now
                    y = y + c[tile][mode] * now
                    terms.append(z * now)
                terms.append(z * x)
                sums[tile] = terms if i == 0 else [a + b for a, b in zip(sums[tile], terms)]
                y_s[spot, strided(i), :] = y
        for tile in range(tiles):
            here = slice(tile * LANES, (tile + 1) * LANES)
            for mode in range(modes + 1):
                rsend[block, mode:mode + 1, here] = jnp.sum(sums[tile][mode], axis=0, keepdims=True)
            rsend[block, modes + 1:, here] = jnp.zeros((modes - 1, LANES), F32)

    def backward_pass(block):
        d = rows_of(decay, block, modes)
        c = rows_of(coef, block, modes)
        sk = rows_of(skip, block, 1)
        back = states_of(modes, block)
        for i in reversed(range(steps)):
            for tile in range(tiles):
                spot = block * tiles + tile
                z = z_s[spot, strided(i), :]
                u = sk[tile][0] * z
                for mode in range(modes):
                    now = d[tile][mode] * back[tile][mode] + z
                    back[tile][mode] = now
                    u = u + c[tile][mode] * now
                u_s[spot, strided(i), :] = u

    def send_sums(block):
        @pl.when(block * stride != me)
        def _():
            sums_copy(block).start()

        @pl.when(block * stride == me)
        def _():
            rgath[me] = rsend[block]

    def owner_scan():
        peers(lambda peer: remote(
            gath.at[peer], gath.at[peer], s1s.at[0], s1r.at[peer], peer).wait_recv())
        d_rows = power(decay[:, lanes_of(own)], rows)

        def forward(p, total):
            ret[p, 0:modes, :] = total
            return d_rows * total + gath[p, 0:modes, :]

        def backward(p, total):
            ret[n - 1 - p, modes:2 * modes, :] = total
            return d_rows * total + gath[n - 1 - p, modes:2 * modes, :]

        zero = jnp.zeros((modes, width), F32)
        lax.fori_loop(0, n, forward, zero, unroll=n <= 16)
        lax.fori_loop(0, n, backward, zero, unroll=n <= 16)
        carry[own] = ret[me]
        peers(lambda peer: return_copy(peer).start())

    def owner_sums():
        peers(lambda peer: remote(
            rgath.at[peer], rgath.at[peer], s3s.at[0], s3r.at[peer], peer).wait_recv())

        def add(p, total):
            return (
                total[0] + rgath[p],
                total[1] + gath[p, modes:2 * modes, :] * ret[p, 0:modes, :],
            )

        whole, cross = lax.fori_loop(
            0, n, add,
            (jnp.zeros((2 * modes, width), F32), jnp.zeros((modes, width), F32)),
            unroll=n <= 16,
        )
        d_all = decay[:, lanes_of(own)]
        spread = jnp.sqrt((1.0 - d_all) * (1.0 + d_all))
        rtot[own, 0:modes, :] = (whole[0:modes] + d_all * cross) * (spread * scale)
        rtot[own, modes:2 * modes, :] = whole[modes:2 * modes] * scale
        peers(lambda peer: total_copy(peer).start())

    first_pass(block_of(0))
    pl.semaphore_wait(barrier, n - 1)
    send_ends(block_of(0))

    @pl.loop(1, m)
    def _(step):
        block = block_of(step)
        first_pass(block)
        send_ends(block)

    @pl.loop(0, m)
    def _(step):
        block = block_of(step)
        forward_pass(block)
        send_sums(block)

    as_owner(owner_scan)
    late = m - m // 4

    @pl.loop(0, late)
    def _(step):
        backward_pass(block_of(step))

    as_owner(owner_sums)

    @pl.loop(late, m)
    def _(step):
        backward_pass(block_of(step))

    for block in range(m):
        @pl.when(block * stride != me)
        def _():
            remote(carry.at[block], carry.at[block], s2s.at[0], s2r.at[block], me).wait_recv()
            remote(rtot.at[block], rtot.at[block], s4s.at[0], s4r.at[block], me).wait_recv()
            ends_copy(block).wait_send()
            sums_copy(block).wait_send()

        at = slice(block * width, (block + 1) * width)
        res_ref[:, at] = rtot[block, 0:modes, :]
        skipg_ref[:, at] = rtot[block, modes:modes + 1, :]
        carried[block] = carry[block]

    def sent():
        def one(peer):
            return_copy(peer).wait_send()
            total_copy(peer).wait_send()

        peers(one)

    as_owner(sent)


def last_kernel(
    m,
    q_in, k_in, v_in, g_in, y_s, u_s, decay, coef, carried, res_ref, skipg_ref,
    out_hbm, dq_hbm, dk_hbm, dv_hbm, res_hbm, skipg_hbm,
    out_v, dq_v, dk_v, dv_v, out_sem, small_sem,
):
    rows, width = q_in.shape[1:]
    tiles = width // LANES
    modes = decay.shape[0]
    steps = rows // SEGS
    hbm_out = (out_hbm, dq_hbm, dk_hbm, dv_hbm)
    vmem_out = (out_v, dq_v, dk_v, dv_v)

    def lanes_of(block, tile):
        return pl.ds(pl.multiple_of(block * width + tile * LANES, LANES), LANES)

    def row(ref, mode, block, tile):
        return jnp.broadcast_to(ref[mode:mode + 1, lanes_of(block, tile)], (SEGS, LANES))

    def padded(first, count):
        return pl.ds(first + first // steps, count)

    def store_copy(index, block):
        return pltpu.make_async_copy(
            vmem_out[index].at[block],
            hbm_out[index].at[:, pl.ds(pl.multiple_of(block * width, LANES), width)],
            out_sem.at[index, block],
        )

    small = [
        pltpu.make_async_copy(res_ref, res_hbm, small_sem.at[0]),
        pltpu.make_async_copy(skipg_ref, skipg_hbm, small_sem.at[1]),
    ]
    for copy in small:
        copy.start()

    place = lax.broadcasted_iota(jnp.int32, (SEGS, LANES), 0)
    bits = [(place & (1 << bit)) != 0 for bit in range(3)]

    def last_pass(block):
        for tile in range(tiles):
            spot = block * tiles + tile
            here = slice(tile * LANES, (tile + 1) * LANES)
            fall = []
            fore = []
            aft = []
            for mode in range(modes):
                base = row(decay, mode, block, tile)
                weight = row(coef, mode, block, tile) * base
                up = weight * jnp.broadcast_to(carried[block, mode:mode + 1, here], (SEGS, LANES))
                down = weight * jnp.broadcast_to(
                    carried[block, modes + mode:modes + mode + 1, here], (SEGS, LANES))
                for bit in bits:
                    up = jnp.where(bit, up * base, up)
                    down = jnp.where(bit, down, down * base)
                    base = base * base
                fall.append(base)
                fore.append(up)
                aft.append(down)
            for pair in range(rows // 16):
                parts = []
                for half in range(2):
                    at = padded(pair * 16 + half * 8, 8)
                    parts.append(y_s[spot, at, :] + ((fore[0] + fore[1]) + (fore[2] + fore[3])))
                    fore = [value * rate for value, rate in zip(fore, fall)]
                mixed = jnp.concatenate(parts, axis=0)
                at = slice(pair * 16, pair * 16 + 16)
                out_v[block, at, here] = (q_in[block, at, here].astype(F32) * mixed).astype(jnp.bfloat16)
                dq_v[block, at, here] = (g_in[block, at, here].astype(F32) * mixed).astype(jnp.bfloat16)
                pair = rows // 16 - 1 - pair
                parts = []
                for half in (1, 0):
                    at = padded(pair * 16 + half * 8, 8)
                    parts.append(u_s[spot, at, :] + ((aft[0] + aft[1]) + (aft[2] + aft[3])))
                    aft = [value * rate for value, rate in zip(aft, fall)]
                mixed = jnp.concatenate(parts[::-1], axis=0)
                at = slice(pair * 16, pair * 16 + 16)
                dk_v[block, at, here] = (v_in[block, at, here].astype(F32) * mixed).astype(jnp.bfloat16)
                dv_v[block, at, here] = (k_in[block, at, here].astype(F32) * mixed).astype(jnp.bfloat16)

    @pl.loop(0, m)
    def _(block):
        last_pass(block)
        for index in range(4):
            store_copy(index, block).start()

    for copy in small:
        copy.wait()

    @pl.loop(0, m)
    def _(block):
        for index in range(4):
            store_copy(index, block).wait()


def local(n, query, key, value, cotangent, decay, residue, skip):
    rows, chans = query.shape
    modes = decay.shape[0]
    m = min(n, chans // LANES)
    width = chans // m
    scale = 1.0 / math.sqrt(rows * n)
    wide = jax.ShapeDtypeStruct((rows, chans), jnp.bfloat16)
    small = (
        jax.ShapeDtypeStruct((modes, chans), F32), jax.ShapeDtypeStruct((1, chans), F32),
    )
    hbm = pl.BlockSpec(memory_space=pltpu.HBM)
    vmem = pl.BlockSpec(memory_space=pltpu.VMEM)
    blocks16 = pltpu.VMEM((m, rows, width), jnp.bfloat16)
    plane = pltpu.VMEM((chans // LANES, rows + SEGS, LANES), F32)
    per_mode = pltpu.VMEM((modes, chans), F32)
    per_chan = pltpu.VMEM((1, chans), F32)
    by_owner = pltpu.VMEM((m, 2 * modes, width), F32)
    by_device = pltpu.VMEM((n, 2 * modes, width), F32)
    dma = pltpu.SemaphoreType.DMA
    held = pl.pallas_call(
        functools.partial(kernel, n, m, scale),
        out_shape=(
            blocks16, blocks16, blocks16, blocks16, plane, plane,
            per_mode, per_mode, by_owner, per_mode, per_chan,
        ),
        in_specs=[hbm] * 7,
        out_specs=(vmem,) * 11,
        scratch_shapes=[
            per_mode, per_chan, plane, plane,
            pltpu.VMEM((width // LANES, 2 * modes * SEGS, LANES), F32),
            pltpu.VMEM((chans // LANES, 2 * modes * SEGS, LANES), F32),
            by_owner, by_device, by_device, by_owner, by_owner, by_device, by_owner,
            dma((4, m)), dma((3,)),
            dma((m,)), dma((n,)), dma((n,)), dma((m,)),
            dma((m,)), dma((n,)), dma((n,)), dma((m,)),
        ],
        compiler_params=pltpu.CompilerParams(
            collective_id=0, has_side_effects=True, vmem_limit_bytes=24 * 1024 * 1024,
        ),
        cost_estimate=pl.CostEstimate(
            flops=60 * rows * chans, bytes_accessed=8 * rows * chans, transcendentals=0
        ),
        name="states",
    )(*[
        pltpu.with_memory_space_constraint(array, pltpu.HBM)
        for array in (query, key, value, cotangent, decay, residue, skip.reshape(1, chans))
    ])
    outs = pl.pallas_call(
        functools.partial(last_kernel, m),
        out_shape=(wide,) * 4 + small,
        in_specs=[vmem] * 11,
        out_specs=(hbm,) * 6,
        scratch_shapes=[blocks16] * 4 + [dma((4, m)), dma((2,))],
        compiler_params=pltpu.CompilerParams(vmem_limit_bytes=24 * 1024 * 1024),
        cost_estimate=pl.CostEstimate(
            flops=30 * rows * chans, bytes_accessed=8 * rows * chans, transcendentals=0
        ),
        name="gates",
    )(*[pltpu.with_memory_space_constraint(array, pltpu.VMEM) for array in held])
    return outs[:5] + (outs[5].reshape(chans),)


def solution(mesh):
    wide = P("ctx", "ch")
    thin = P(None, "ch")
    return jax.shard_map(
        functools.partial(local, mesh.shape["ctx"]),
        mesh=mesh,
        in_specs=(wide, wide, wide, wide, thin, thin, P("ch")),
        out_specs=(wide, wide, wide, wide, thin, P("ch")),
        check_vma=False,
    )
```

```python
import functools
import math

import jax
import jax.numpy as jnp
from jax import lax
from jax.experimental import pallas as pl
from jax.experimental.pallas import tpu as pltpu
from jax.sharding import PartitionSpec as P

LANES = 128
SEGS = 8
F32 = jnp.float32
MESH = pl.DeviceIdType.MESH


def each(low, high, body):
    if high - low <= 16:
        for step in range(low, high):
            body(step)
    else:
        def wrapped(step, carry):
            body(step)
            return carry

        lax.fori_loop(low, high, wrapped, 0)


def power(base, exponent):
    result = None
    while exponent:
        if exponent & 1:
            result = base if result is None else result * base
        exponent >>= 1
        if exponent:
            base = base * base
    return result


def kernel(
    n, m, scale,
    q_hbm, k_hbm, v_hbm, g_hbm, decay_hbm, residue_hbm, skip_hbm,
    q_in, k_in, v_in, g_in, y_s, u_s, decay, coef, carry,
    residue, skip, x_s, z_s, seg, start, mine, gath, ret,
    in_sem, par_sem, s1s, s1r, s2s, s2r,
):
    me = lax.axis_index("ctx")
    rows = q_hbm.shape[0]
    width = q_hbm.shape[1] // m
    tiles = width // LANES
    modes = decay_hbm.shape[0]
    steps = rows // SEGS
    stride = n // m
    own = me // stride
    hbm_in = (q_hbm, k_hbm, v_hbm, g_hbm)
    vmem_in = (q_in, k_in, v_in, g_in)

    def block_of(step):
        return lax.rem(me + 1 + step, m)

    def lanes_of(block, tile=None):
        if tile is None:
            return pl.ds(pl.multiple_of(block * width, LANES), width)
        return pl.ds(pl.multiple_of(block * width + tile * LANES, LANES), LANES)

    def load_copy(index, block):
        return pltpu.make_async_copy(
            hbm_in[index].at[:, lanes_of(block)], vmem_in[index].at[block],
            in_sem.at[index, block],
        )

    params = [
        pltpu.make_async_copy(decay_hbm, decay, par_sem.at[0]),
        pltpu.make_async_copy(residue_hbm, residue, par_sem.at[1]),
        pltpu.make_async_copy(skip_hbm, skip, par_sem.at[2]),
    ]

    def remote(src, dst, send_sem, recv_sem, device):
        return pltpu.make_async_remote_copy(
            src_ref=src, dst_ref=dst, send_sem=send_sem, recv_sem=recv_sem,
            device_id={"ctx": device}, device_id_type=MESH,
        )

    def ends_copy(block):
        return remote(mine.at[block], gath.at[me], s1s.at[block], s1r.at[me], block * stride)

    def return_copy(peer):
        return remote(ret.at[peer], carry.at[own], s2s.at[peer], s2r.at[own], peer)

    def as_owner(body):
        if stride == 1:
            body()
        else:
            pl.when(lax.rem(me, stride) == 0)(body)

    def peers(body):
        each(1, n, lambda r: body(lax.rem(me + r, n)))

    def row(ref, mode, block, tile):
        return jnp.broadcast_to(ref[mode:mode + 1, lanes_of(block, tile)], (SEGS, LANES))

    def strided(index):
        return pl.ds(index, SEGS, stride=steps + 1)

    def padded(first, count):
        return pl.ds(first + first // steps, count)

    barrier = pltpu.get_barrier_semaphore()
    for copy in params:
        copy.start()
    for step in range(m):
        for index in range(4):
            load_copy(index, block_of(step)).start()
    peers(lambda peer: pl.semaphore_signal(
        barrier, inc=1, device_id={"ctx": peer}, device_id_type=MESH))
    for copy in params:
        copy.wait()

    def first_pass(block):
        for index in range(4):
            load_copy(index, block).wait()
        d = []
        for tile in range(tiles):
            spot = block * tiles + tile
            here = slice(tile * LANES, (tile + 1) * LANES)
            for j in range(SEGS):
                at = slice(j * steps, (j + 1) * steps)
                to = padded(j * steps, steps)
                x_s[spot, to, :] = k_in[block, at, here].astype(F32) * v_in[block, at, here].astype(F32)
                z_s[spot, to, :] = g_in[block, at, here].astype(F32) * q_in[block, at, here].astype(F32)
            d.append([row(decay, mode, block, tile) for mode in range(modes)])
        tail = [[None] * modes for _ in range(tiles)]
        head = [[None] * modes for _ in range(tiles)]
        sums = [None] * tiles
        for i in range(steps):
            for tile in range(tiles):
                spot = block * tiles + tile
                x = x_s[spot, strided(i), :]
                z = z_s[spot, strided(steps - 1 - i), :]
                beside = z_s[spot, strided(i), :]
                for mode in range(modes):
                    tail[tile][mode] = x if i == 0 else d[tile][mode] * tail[tile][mode] + x
                    head[tile][mode] = z if i == 0 else d[tile][mode] * head[tile][mode] + z
                terms = [beside * now for now in tail[tile] + [x]]
                sums[tile] = terms if i == 0 else [a + b for a, b in zip(sums[tile], terms)]
        for tile in range(tiles):
            for mode in range(modes):
                seg[tile, mode * SEGS:(mode + 1) * SEGS, :] = tail[tile][mode]
                seg[tile, (modes + mode) * SEGS:(modes + mode + 1) * SEGS, :] = head[tile][mode]
        for tile in range(tiles):
            spot = block * tiles + tile
            here = slice(tile * LANES, (tile + 1) * LANES)
            d_all = decay[:, lanes_of(block, tile)]
            spread = jnp.sqrt((1.0 - d_all) * (1.0 + d_all))
            coef[:, lanes_of(block, tile)] = residue[:, lanes_of(block, tile)] * spread
            d_seg = power(d_all, steps)
            up = jnp.zeros((modes, LANES), F32)
            down = jnp.zeros((modes, LANES), F32)
            for j in range(SEGS):
                at = pl.ds(j, modes, stride=SEGS)
                start[spot, at, :] = up
                up = d_seg * up + seg[tile, at, :]
                at = pl.ds(modes * SEGS + SEGS - 1 - j, modes, stride=SEGS)
                start[spot, at, :] = down
                down = d_seg * down + seg[tile, at, :]
            mine[block, 0:modes, here] = up
            mine[block, modes:2 * modes, here] = down
            for mode in range(modes + 1):
                total = sums[tile][mode]
                if mode < modes:
                    begun = start[spot, mode * SEGS:(mode + 1) * SEGS, :]
                    total = total + d[tile][mode] * head[tile][mode] * begun
                at = 2 * modes + mode
                mine[block, at:at + 1, here] = jnp.sum(total, axis=0, keepdims=True)
            mine[block, 3 * modes + 1:, here] = jnp.zeros((modes - 1, LANES), F32)

    def send_ends(block):
        @pl.when(block * stride != me)
        def _():
            ends_copy(block).start()

        @pl.when(block * stride == me)
        def _():
            gath[me] = mine[block]

    def rows_of(ref, block, count):
        return [[row(ref, mode, block, tile) for mode in range(count)] for tile in range(tiles)]

    def states_of(first, block):
        return [
            [
                start[block * tiles + tile, (first + mode) * SEGS:(first + mode + 1) * SEGS, :]
                for mode in range(modes)
            ]
            for tile in range(tiles)
        ]

    def middle_pass(block):
        d = rows_of(decay, block, modes)
        c = rows_of(coef, block, modes)
        sk = rows_of(skip, block, 1)
        state = states_of(0, block)
        back = states_of(modes, block)
        for i in range(steps):
            for tile in range(tiles):
                spot = block * tiles + tile
                x = x_s[spot, strided(i), :]
                z = z_s[spot, strided(steps - 1 - i), :]
                y = sk[tile][0] * x
                u = sk[tile][0] * z
                for mode in range(modes):
                    state[tile][mode] = d[tile][mode] * state[tile][mode] + x
                    back[tile][mode] = d[tile][mode] * back[tile][mode] + z
                    y = y + c[tile][mode] * state[tile][mode]
                    u = u + c[tile][mode] * back[tile][mode]
                y_s[spot, strided(i), :] = y
                u_s[spot, strided(steps - 1 - i), :] = u

    def owner_scan():
        peers(lambda peer: remote(
            gath.at[peer], gath.at[peer], s1s.at[0], s1r.at[peer], peer).wait_recv())
        d_rows = power(decay[:, lanes_of(own)], rows)

        def forward(p, total):
            ret[p, 0:modes, :] = total
            return d_rows * total + gath[p, 0:modes, :]

        def backward(p, total):
            ret[n - 1 - p, modes:2 * modes, :] = total
            return d_rows * total + gath[n - 1 - p, modes:2 * modes, :]

        zero = jnp.zeros((modes, width), F32)
        lax.fori_loop(0, n, forward, zero, unroll=n <= 16)
        lax.fori_loop(0, n, backward, zero, unroll=n <= 16)

        def add(p, total):
            return (
                total[0] + gath[p, 2 * modes:, :],
                total[1] + gath[p, modes:2 * modes, :] * ret[p, 0:modes, :],
            )

        whole, cross = lax.fori_loop(
            0, n, add, (jnp.zeros((2 * modes, width), F32), zero), unroll=n <= 16)
        d_all = decay[:, lanes_of(own)]
        spread = jnp.sqrt((1.0 - d_all) * (1.0 + d_all))
        weights = (whole[0:modes] + d_all * cross) * (spread * scale)
        skips = whole[modes:] * scale

        def put(p):
            ret[p, 2 * modes:3 * modes, :] = weights
            ret[p, 3 * modes:, :] = skips

        each(0, n, put)
        carry[own] = ret[me]
        peers(lambda peer: return_copy(peer).start())

    first_pass(block_of(0))
    pl.semaphore_wait(barrier, n - 1)
    send_ends(block_of(0))

    @pl.loop(1, m)
    def _(step):
        block = block_of(step)
        first_pass(block)
        send_ends(block)

    half = m // 2

    @pl.loop(0, half)
    def _(step):
        middle_pass(block_of(step))

    as_owner(owner_scan)

    @pl.loop(half, m)
    def _(step):
        middle_pass(block_of(step))

    for block in range(m):
        @pl.when(block * stride != me)
        def _():
            ends_copy(block).wait_send()
            remote(carry.at[block], carry.at[block], s2s.at[0], s2r.at[block], me).wait_recv()

    as_owner(lambda: peers(lambda peer: return_copy(peer).wait_send()))


def last_kernel(
    m,
    q_in, k_in, v_in, g_in, y_s, u_s, decay, coef, carried,
    out_hbm, dq_hbm, dk_hbm, dv_hbm, res_hbm, skipg_hbm,
    out_v, dq_v, dk_v, dv_v, res_ref, skipg_ref, out_sem, small_sem,
):
    rows, width = q_in.shape[1:]
    tiles = width // LANES
    modes = decay.shape[0]
    steps = rows // SEGS
    hbm_out = (out_hbm, dq_hbm, dk_hbm, dv_hbm)
    vmem_out = (out_v, dq_v, dk_v, dv_v)

    def lanes_of(block, tile):
        return pl.ds(pl.multiple_of(block * width + tile * LANES, LANES), LANES)

    def row(ref, mode, block, tile):
        return jnp.broadcast_to(ref[mode:mode + 1, lanes_of(block, tile)], (SEGS, LANES))

    def padded(first, count):
        return pl.ds(first + first // steps, count)

    def store_copy(index, block):
        return pltpu.make_async_copy(
            vmem_out[index].at[block],
            hbm_out[index].at[:, pl.ds(pl.multiple_of(block * width, LANES), width)],
            out_sem.at[index, block],
        )

    for block in range(m):
        at = slice(block * width, (block + 1) * width)
        res_ref[:, at] = carried[block, 2 * modes:3 * modes, :]
        skipg_ref[:, at] = carried[block, 3 * modes:3 * modes + 1, :]
    small = [
        pltpu.make_async_copy(res_ref, res_hbm, small_sem.at[0]),
        pltpu.make_async_copy(skipg_ref, skipg_hbm, small_sem.at[1]),
    ]
    for copy in small:
        copy.start()

    place = lax.broadcasted_iota(jnp.int32, (SEGS, LANES), 0)
    bits = [(place & (1 << bit)) != 0 for bit in range(3)]

    def last_pass(block):
        for tile in range(tiles):
            spot = block * tiles + tile
            here = slice(tile * LANES, (tile + 1) * LANES)
            fall = []
            fore = []
            aft = []
            for mode in range(modes):
                base = row(decay, mode, block, tile)
                weight = row(coef, mode, block, tile) * base
                up = weight * jnp.broadcast_to(carried[block, mode:mode + 1, here], (SEGS, LANES))
                down = weight * jnp.broadcast_to(
                    carried[block, modes + mode:modes + mode + 1, here], (SEGS, LANES))
                for bit in bits:
                    up = jnp.where(bit, up * base, up)
                    down = jnp.where(bit, down, down * base)
                    base = base * base
                fall.append(base)
                fore.append(up)
                aft.append(down)
            for pair in range(rows // 16):
                parts = []
                for half in range(2):
                    at = padded(pair * 16 + half * 8, 8)
                    parts.append(y_s[spot, at, :] + ((fore[0] + fore[1]) + (fore[2] + fore[3])))
                    fore = [value * rate for value, rate in zip(fore, fall)]
                mixed = jnp.concatenate(parts, axis=0)
                at = slice(pair * 16, pair * 16 + 16)
                out_v[block, at, here] = (q_in[block, at, here].astype(F32) * mixed).astype(jnp.bfloat16)
                dq_v[block, at, here] = (g_in[block, at, here].astype(F32) * mixed).astype(jnp.bfloat16)
                pair = rows // 16 - 1 - pair
                parts = []
                for half in (1, 0):
                    at = padded(pair * 16 + half * 8, 8)
                    parts.append(u_s[spot, at, :] + ((aft[0] + aft[1]) + (aft[2] + aft[3])))
                    aft = [value * rate for value, rate in zip(aft, fall)]
                mixed = jnp.concatenate(parts[::-1], axis=0)
                at = slice(pair * 16, pair * 16 + 16)
                dk_v[block, at, here] = (v_in[block, at, here].astype(F32) * mixed).astype(jnp.bfloat16)
                dv_v[block, at, here] = (k_in[block, at, here].astype(F32) * mixed).astype(jnp.bfloat16)

    @pl.loop(0, m)
    def _(block):
        last_pass(block)
        for index in range(4):
            store_copy(index, block).start()

    for copy in small:
        copy.wait()

    @pl.loop(0, m)
    def _(block):
        for index in range(4):
            store_copy(index, block).wait()


def local(n, query, key, value, cotangent, decay, residue, skip):
    rows, chans = query.shape
    modes = decay.shape[0]
    m = min(n, chans // LANES)
    width = chans // m
    scale = 1.0 / math.sqrt(rows * n)
    wide = jax.ShapeDtypeStruct((rows, chans), jnp.bfloat16)
    small = (
        jax.ShapeDtypeStruct((modes, chans), F32), jax.ShapeDtypeStruct((1, chans), F32),
    )
    hbm = pl.BlockSpec(memory_space=pltpu.HBM)
    vmem = pl.BlockSpec(memory_space=pltpu.VMEM)
    blocks16 = pltpu.VMEM((m, rows, width), jnp.bfloat16)
    plane = pltpu.VMEM((chans // LANES, rows + SEGS, LANES), F32)
    per_mode = pltpu.VMEM((modes, chans), F32)
    per_chan = pltpu.VMEM((1, chans), F32)
    by_owner = pltpu.VMEM((m, 4 * modes, width), F32)
    by_device = pltpu.VMEM((n, 4 * modes, width), F32)
    dma = pltpu.SemaphoreType.DMA
    held = pl.pallas_call(
        functools.partial(kernel, n, m, scale),
        out_shape=(
            blocks16, blocks16, blocks16, blocks16, plane, plane,
            per_mode, per_mode, by_owner,
        ),
        in_specs=[hbm] * 7,
        out_specs=(vmem,) * 9,
        scratch_shapes=[
            per_mode, per_chan, plane, plane,
            pltpu.VMEM((width // LANES, 2 * modes * SEGS, LANES), F32),
            pltpu.VMEM((chans // LANES, 2 * modes * SEGS, LANES), F32),
            by_owner, by_device, by_device,
            dma((4, m)), dma((3,)),
            dma((m,)), dma((n,)), dma((n,)), dma((m,)),
        ],
        compiler_params=pltpu.CompilerParams(
            collective_id=0, has_side_effects=True, vmem_limit_bytes=24 * 1024 * 1024,
        ),
        cost_estimate=pl.CostEstimate(
            flops=60 * rows * chans, bytes_accessed=8 * rows * chans, transcendentals=0
        ),
        name="states",
    )(*[
        pltpu.with_memory_space_constraint(array, pltpu.HBM)
        for array in (query, key, value, cotangent, decay, residue, skip.reshape(1, chans))
    ])
    outs = pl.pallas_call(
        functools.partial(last_kernel, m),
        out_shape=(wide,) * 4 + small,
        in_specs=[vmem] * 9,
        out_specs=(hbm,) * 6,
        scratch_shapes=[blocks16] * 4 + [per_mode, per_chan, dma((4, m)), dma((2,))],
        compiler_params=pltpu.CompilerParams(vmem_limit_bytes=24 * 1024 * 1024),
        cost_estimate=pl.CostEstimate(
            flops=30 * rows * chans, bytes_accessed=8 * rows * chans, transcendentals=0
        ),
        name="gates",
    )(*[pltpu.with_memory_space_constraint(array, pltpu.VMEM) for array in held])
    return outs[:5] + (outs[5].reshape(chans),)


def solution(mesh):
    wide = P("ctx", "ch")
    thin = P(None, "ch")
    return jax.shard_map(
        functools.partial(local, mesh.shape["ctx"]),
        mesh=mesh,
        in_specs=(wide, wide, wide, wide, thin, thin, P("ch")),
        out_specs=(wide, wide, wide, wide, thin, P("ch")),
        check_vma=False,
    )
```

```python
import functools
import math

import jax
import jax.numpy as jnp
from jax import lax
from jax.experimental import pallas as pl
from jax.experimental.pallas import tpu as pltpu
from jax.sharding import PartitionSpec as P

LANES = 128
SEGS = 8
F32 = jnp.float32
MESH = pl.DeviceIdType.MESH


def each(low, high, body):
    if high - low <= 16:
        for step in range(low, high):
            body(step)
    else:
        def wrapped(step, carry):
            body(step)
            return carry

        lax.fori_loop(low, high, wrapped, 0)


def far_first(index, size, step):
    if size % 2:
        return lax.rem(index + 1 + step, size)
    half = size // 2
    later = step // half
    return lax.rem(index // half + 1 + later, 2) * half + lax.rem(index + step + later, half)


def power(base, exponent):
    result = None
    while exponent:
        if exponent & 1:
            result = base if result is None else result * base
        exponent >>= 1
        if exponent:
            base = base * base
    return result


def kernel(
    n, m, scale,
    q_hbm, k_hbm, v_hbm, g_hbm, decay_hbm, residue_hbm, skip_hbm,
    q_in, k_in, v_in, g_in, y_s, u_s, decay, coef, carry,
    residue, skip, x_s, z_s, seg, start, mine, gath, ret,
    in_sem, par_sem, s1s, s1r, s2s, s2r,
):
    me = lax.axis_index("ctx")
    rows = q_hbm.shape[0]
    width = q_hbm.shape[1] // m
    tiles = width // LANES
    modes = decay_hbm.shape[0]
    steps = rows // SEGS
    stride = n // m
    own = me // stride
    hbm_in = (q_hbm, k_hbm, v_hbm, g_hbm)
    vmem_in = (q_in, k_in, v_in, g_in)

    def block_of(step):
        return far_first(own, m, step)

    def lanes_of(block, tile=None):
        if tile is None:
            return pl.ds(pl.multiple_of(block * width, LANES), width)
        return pl.ds(pl.multiple_of(block * width + tile * LANES, LANES), LANES)

    def load_copy(index, block):
        return pltpu.make_async_copy(
            hbm_in[index].at[:, lanes_of(block)], vmem_in[index].at[block],
            in_sem.at[index, block],
        )

    params = [
        pltpu.make_async_copy(decay_hbm, decay, par_sem.at[0]),
        pltpu.make_async_copy(residue_hbm, residue, par_sem.at[1]),
        pltpu.make_async_copy(skip_hbm, skip, par_sem.at[2]),
    ]

    def remote(src, dst, send_sem, recv_sem, device):
        return pltpu.make_async_remote_copy(
            src_ref=src, dst_ref=dst, send_sem=send_sem, recv_sem=recv_sem,
            device_id={"ctx": device}, device_id_type=MESH,
        )

    def ends_copy(block):
        return remote(mine.at[block], gath.at[me], s1s.at[block], s1r.at[me], block * stride)

    def return_copy(peer):
        return remote(ret.at[peer], carry.at[own], s2s.at[peer], s2r.at[own], peer)

    def as_owner(body):
        if stride == 1:
            body()
        else:
            pl.when(lax.rem(me, stride) == 0)(body)

    def peers(body):
        each(0, n - 1, lambda step: body(far_first(me, n, step)))

    def row(ref, mode, block, tile):
        return jnp.broadcast_to(ref[mode:mode + 1, lanes_of(block, tile)], (SEGS, LANES))

    def strided(index):
        return pl.ds(index, SEGS, stride=steps + 1)

    def padded(first, count):
        return pl.ds(first + first // steps, count)

    barrier = pltpu.get_barrier_semaphore()
    peers(lambda peer: pl.semaphore_signal(
        barrier, inc=1, device_id={"ctx": peer}, device_id_type=MESH))
    for copy in params:
        copy.start()
    for step in range(m):
        for index in range(4):
            load_copy(index, block_of(step)).start()
    for copy in params:
        copy.wait()

    def first_pass(block):
        for index in range(4):
            load_copy(index, block).wait()
        d = []
        for tile in range(tiles):
            spot = block * tiles + tile
            here = slice(tile * LANES, (tile + 1) * LANES)
            for j in range(SEGS):
                at = slice(j * steps, (j + 1) * steps)
                to = padded(j * steps, steps)
                x_s[spot, to, :] = k_in[block, at, here].astype(F32) * v_in[block, at, here].astype(F32)
                z_s[spot, to, :] = g_in[block, at, here].astype(F32) * q_in[block, at, here].astype(F32)
            d.append([row(decay, mode, block, tile) for mode in range(modes)])
        tail = [[None] * modes for _ in range(tiles)]
        head = [[None] * modes for _ in range(tiles)]
        sums = [None] * tiles
        for i in range(steps):
            for tile in range(tiles):
                spot = block * tiles + tile
                x = x_s[spot, strided(i), :]
                z = z_s[spot, strided(steps - 1 - i), :]
                beside = z_s[spot, strided(i), :]
                for mode in range(modes):
                    tail[tile][mode] = x if i == 0 else d[tile][mode] * tail[tile][mode] + x
                    head[tile][mode] = z if i == 0 else d[tile][mode] * head[tile][mode] + z
                terms = [beside * now for now in tail[tile] + [x]]
                sums[tile] = terms if i == 0 else [a + b for a, b in zip(sums[tile], terms)]
        for tile in range(tiles):
            for mode in range(modes):
                seg[tile, mode * SEGS:(mode + 1) * SEGS, :] = tail[tile][mode]
                seg[tile, (modes + mode) * SEGS:(modes + mode + 1) * SEGS, :] = head[tile][mode]
        for tile in range(tiles):
            spot = block * tiles + tile
            here = slice(tile * LANES, (tile + 1) * LANES)
            d_all = decay[:, lanes_of(block, tile)]
            spread = jnp.sqrt((1.0 - d_all) * (1.0 + d_all))
            coef[:, lanes_of(block, tile)] = residue[:, lanes_of(block, tile)] * spread
            d_seg = power(d_all, steps)
            up = jnp.zeros((modes, LANES), F32)
            down = jnp.zeros((modes, LANES), F32)
            for j in range(SEGS):
                at = pl.ds(j, modes, stride=SEGS)
                start[spot, at, :] = up
                up = d_seg * up + seg[tile, at, :]
                at = pl.ds(modes * SEGS + SEGS - 1 - j, modes, stride=SEGS)
                start[spot, at, :] = down
                down = d_seg * down + seg[tile, at, :]
            mine[block, 0:modes, here] = up
            mine[block, modes:2 * modes, here] = down
            for mode in range(modes + 1):
                total = sums[tile][mode]
                if mode < modes:
                    begun = start[spot, mode * SEGS:(mode + 1) * SEGS, :]
                    total = total + d[tile][mode] * head[tile][mode] * begun
                at = 2 * modes + mode
                mine[block, at:at + 1, here] = jnp.sum(total, axis=0, keepdims=True)
            mine[block, 3 * modes + 1:, here] = jnp.zeros((modes - 1, LANES), F32)

    def send_ends(block):
        @pl.when(block * stride != me)
        def _():
            ends_copy(block).start()

        @pl.when(block * stride == me)
        def _():
            gath[me] = mine[block]

    def rows_of(ref, block, count):
        return [[row(ref, mode, block, tile) for mode in range(count)] for tile in range(tiles)]

    def states_of(first, block):
        return [
            [
                start[block * tiles + tile, (first + mode) * SEGS:(first + mode + 1) * SEGS, :]
                for mode in range(modes)
            ]
            for tile in range(tiles)
        ]

    def middle_pass(block):
        d = rows_of(decay, block, modes)
        c = rows_of(coef, block, modes)
        sk = rows_of(skip, block, 1)
        state = states_of(0, block)
        back = states_of(modes, block)
        for i in range(steps):
            for tile in range(tiles):
                spot = block * tiles + tile
                x = x_s[spot, strided(i), :]
                z = z_s[spot, strided(steps - 1 - i), :]
                y = sk[tile][0] * x
                u = sk[tile][0] * z
                for mode in range(modes):
                    state[tile][mode] = d[tile][mode] * state[tile][mode] + x
                    back[tile][mode] = d[tile][mode] * back[tile][mode] + z
                    y = y + c[tile][mode] * state[tile][mode]
                    u = u + c[tile][mode] * back[tile][mode]
                y_s[spot, strided(i), :] = y
                u_s[spot, strided(steps - 1 - i), :] = u

    def owner_scan():
        peers(lambda peer: remote(
            gath.at[peer], gath.at[peer], s1s.at[0], s1r.at[peer], peer).wait_recv())
        d_rows = power(decay[:, lanes_of(own)], rows)

        def forward(p, total):
            ret[p, 0:modes, :] = total
            return d_rows * total + gath[p, 0:modes, :]

        def backward(p, total):
            ret[n - 1 - p, modes:2 * modes, :] = total
            return d_rows * total + gath[n - 1 - p, modes:2 * modes, :]

        zero = jnp.zeros((modes, width), F32)
        lax.fori_loop(0, n, forward, zero, unroll=n <= 16)
        lax.fori_loop(0, n, backward, zero, unroll=n <= 16)

        def add(p, total):
            return (
                total[0] + gath[p, 2 * modes:, :],
                total[1] + gath[p, modes:2 * modes, :] * ret[p, 0:modes, :],
            )

        whole, cross = lax.fori_loop(
            0, n, add, (jnp.zeros((2 * modes, width), F32), zero), unroll=n <= 16)
        d_all = decay[:, lanes_of(own)]
        spread = jnp.sqrt((1.0 - d_all) * (1.0 + d_all))
        weights = (whole[0:modes] + d_all * cross) * (spread * scale)
        skips = whole[modes:] * scale

        def put(p):
            ret[p, 2 * modes:3 * modes, :] = weights
            ret[p, 3 * modes:, :] = skips

        each(0, n, put)
        carry[own] = ret[me]
        peers(lambda peer: return_copy(peer).start())

    first_pass(block_of(0))
    pl.semaphore_wait(barrier, n - 1)
    send_ends(block_of(0))

    @pl.loop(1, m)
    def _(step):
        block = block_of(step)
        first_pass(block)
        send_ends(block)

    half = m // 2

    @pl.loop(0, half)
    def _(step):
        middle_pass(block_of(step))

    as_owner(owner_scan)

    @pl.loop(half, m)
    def _(step):
        middle_pass(block_of(step))

    for block in range(m):
        @pl.when(block * stride != me)
        def _():
            ends_copy(block).wait_send()
            remote(carry.at[block], carry.at[block], s2s.at[0], s2r.at[block], me).wait_recv()

    as_owner(lambda: peers(lambda peer: return_copy(peer).wait_send()))


def last_kernel(
    m,
    q_in, k_in, v_in, g_in, y_s, u_s, decay, coef, carried,
    out_hbm, dq_hbm, dk_hbm, dv_hbm, res_hbm, skipg_hbm,
    out_v, dq_v, dk_v, dv_v, res_ref, skipg_ref, out_sem, small_sem,
):
    rows, width = q_in.shape[1:]
    tiles = width // LANES
    modes = decay.shape[0]
    steps = rows // SEGS
    hbm_out = (out_hbm, dq_hbm, dk_hbm, dv_hbm)
    vmem_out = (out_v, dq_v, dk_v, dv_v)

    def lanes_of(block, tile):
        return pl.ds(pl.multiple_of(block * width + tile * LANES, LANES), LANES)

    def row(ref, mode, block, tile):
        return jnp.broadcast_to(ref[mode:mode + 1, lanes_of(block, tile)], (SEGS, LANES))

    def padded(first, count):
        return pl.ds(first + first // steps, count)

    def store_copy(index, block):
        return pltpu.make_async_copy(
            vmem_out[index].at[block],
            hbm_out[index].at[:, pl.ds(pl.multiple_of(block * width, LANES), width)],
            out_sem.at[index, block],
        )

    for block in range(m):
        at = slice(block * width, (block + 1) * width)
        res_ref[:, at] = carried[block, 2 * modes:3 * modes, :]
        skipg_ref[:, at] = carried[block, 3 * modes:3 * modes + 1, :]
    small = [
        pltpu.make_async_copy(res_ref, res_hbm, small_sem.at[0]),
        pltpu.make_async_copy(skipg_ref, skipg_hbm, small_sem.at[1]),
    ]
    for copy in small:
        copy.start()

    place = lax.broadcasted_iota(jnp.int32, (SEGS, LANES), 0)
    bits = [(place & (1 << bit)) != 0 for bit in range(3)]

    def last_pass(block):
        for tile in range(tiles):
            spot = block * tiles + tile
            here = slice(tile * LANES, (tile + 1) * LANES)
            fall = []
            fore = []
            aft = []
            for mode in range(modes):
                base = row(decay, mode, block, tile)
                weight = row(coef, mode, block, tile) * base
                up = weight * jnp.broadcast_to(carried[block, mode:mode + 1, here], (SEGS, LANES))
                down = weight * jnp.broadcast_to(
                    carried[block, modes + mode:modes + mode + 1, here], (SEGS, LANES))
                for bit in bits:
                    up = jnp.where(bit, up * base, up)
                    down = jnp.where(bit, down, down * base)
                    base = base * base
                fall.append(base)
                fore.append(up)
                aft.append(down)
            for pair in range(rows // 16):
                parts = []
                for half in range(2):
                    at = padded(pair * 16 + half * 8, 8)
                    parts.append(y_s[spot, at, :] + ((fore[0] + fore[1]) + (fore[2] + fore[3])))
                    fore = [value * rate for value, rate in zip(fore, fall)]
                mixed = jnp.concatenate(parts, axis=0)
                at = slice(pair * 16, pair * 16 + 16)
                out_v[block, at, here] = (q_in[block, at, here].astype(F32) * mixed).astype(jnp.bfloat16)
                dq_v[block, at, here] = (g_in[block, at, here].astype(F32) * mixed).astype(jnp.bfloat16)
                pair = rows // 16 - 1 - pair
                parts = []
                for half in (1, 0):
                    at = padded(pair * 16 + half * 8, 8)
                    parts.append(u_s[spot, at, :] + ((aft[0] + aft[1]) + (aft[2] + aft[3])))
                    aft = [value * rate for value, rate in zip(aft, fall)]
                mixed = jnp.concatenate(parts[::-1], axis=0)
                at = slice(pair * 16, pair * 16 + 16)
                dk_v[block, at, here] = (v_in[block, at, here].astype(F32) * mixed).astype(jnp.bfloat16)
                dv_v[block, at, here] = (k_in[block, at, here].astype(F32) * mixed).astype(jnp.bfloat16)

    @pl.loop(0, m)
    def _(block):
        last_pass(block)
        for index in range(4):
            store_copy(index, block).start()

    for copy in small:
        copy.wait()

    @pl.loop(0, m)
    def _(block):
        for index in range(4):
            store_copy(index, block).wait()


def local(n, query, key, value, cotangent, decay, residue, skip):
    rows, chans = query.shape
    modes = decay.shape[0]
    m = min(n, chans // LANES)
    width = chans // m
    scale = 1.0 / math.sqrt(rows * n)
    wide = jax.ShapeDtypeStruct((rows, chans), jnp.bfloat16)
    small = (
        jax.ShapeDtypeStruct((modes, chans), F32), jax.ShapeDtypeStruct((1, chans), F32),
    )
    hbm = pl.BlockSpec(memory_space=pltpu.HBM)
    vmem = pl.BlockSpec(memory_space=pltpu.VMEM)
    blocks16 = pltpu.VMEM((m, rows, width), jnp.bfloat16)
    plane = pltpu.VMEM((chans // LANES, rows + SEGS, LANES), F32)
    per_mode = pltpu.VMEM((modes, chans), F32)
    per_chan = pltpu.VMEM((1, chans), F32)
    by_owner = pltpu.VMEM((m, 4 * modes, width), F32)
    by_device = pltpu.VMEM((n, 4 * modes, width), F32)
    dma = pltpu.SemaphoreType.DMA
    held = pl.pallas_call(
        functools.partial(kernel, n, m, scale),
        out_shape=(
            blocks16, blocks16, blocks16, blocks16, plane, plane,
            per_mode, per_mode, by_owner,
        ),
        in_specs=[hbm] * 7,
        out_specs=(vmem,) * 9,
        scratch_shapes=[
            per_mode, per_chan, plane, plane,
            pltpu.VMEM((width // LANES, 2 * modes * SEGS, LANES), F32),
            pltpu.VMEM((chans // LANES, 2 * modes * SEGS, LANES), F32),
            by_owner, by_device, by_device,
            dma((4, m)), dma((3,)),
            dma((m,)), dma((n,)), dma((n,)), dma((m,)),
        ],
        compiler_params=pltpu.CompilerParams(
            collective_id=0, has_side_effects=True, vmem_limit_bytes=24 * 1024 * 1024,
        ),
        cost_estimate=pl.CostEstimate(
            flops=60 * rows * chans, bytes_accessed=8 * rows * chans, transcendentals=0
        ),
        name="states",
    )(*[
        pltpu.with_memory_space_constraint(array, pltpu.HBM)
        for array in (query, key, value, cotangent, decay, residue, skip.reshape(1, chans))
    ])
    outs = pl.pallas_call(
        functools.partial(last_kernel, m),
        out_shape=(wide,) * 4 + small,
        in_specs=[vmem] * 9,
        out_specs=(hbm,) * 6,
        scratch_shapes=[blocks16] * 4 + [per_mode, per_chan, dma((4, m)), dma((2,))],
        compiler_params=pltpu.CompilerParams(vmem_limit_bytes=24 * 1024 * 1024),
        cost_estimate=pl.CostEstimate(
            flops=30 * rows * chans, bytes_accessed=8 * rows * chans, transcendentals=0
        ),
        name="gates",
    )(*[pltpu.with_memory_space_constraint(array, pltpu.VMEM) for array in held])
    return outs[:5] + (outs[5].reshape(chans),)


def solution(mesh):
    wide = P("ctx", "ch")
    thin = P(None, "ch")
    return jax.shard_map(
        functools.partial(local, mesh.shape["ctx"]),
        mesh=mesh,
        in_specs=(wide, wide, wide, wide, thin, thin, P("ch")),
        out_specs=(wide, wide, wide, wide, thin, P("ch")),
        check_vma=False,
    )
```
